256 devices in a mesh: grp: 8 (over z), seq: 32 (over y, x, core).
Axes of the slice: x: 4, y: 4, z: 8, core: 2. Of those that a mesh axis runs over, the one named last changes fastest.
Arguments:
- queries: bfloat16 [8, 4096, 640], P('grp', 'seq'), may hold values from -140 to 140
- resp_kv: bfloat16 [8, 4096, 256], P('grp', 'seq'), may hold values from -6 to 6
- grad_out: bfloat16 [8, 4096, 640], P('grp', 'seq'), may hold values from -6 to 6
- prompt_kv: bfloat16 [8, 5, 2048, 256], P('grp', None, 'seq'), may hold values from -5 to 5
- resp_inputs: bfloat16 [8, 4096, 5120], P('grp', 'seq'), may hold values from -6 to 6
- prompt_inputs: bfloat16 [8, 5, 2048, 5120], P('grp', None, 'seq'), may hold values from -6 to 6
- prompt_blocks: int32 [8, 8], P('grp'), may hold values from 1 to 32, 136 in all within a row
- response_order: int32 [8, 64], P('grp'), may hold values from 0 to 63, each once within a row
- response_len: int32 [8, 64], P('grp', 'seq'), may hold values from 1 to 64, 2457 in all within a row
Outputs:
- d_queries: bfloat16 [8, 4096, 640], P('grp', 'seq')
- d_resp_kv: bfloat16 [8, 4096, 256], P('grp', 'seq')
- d_prompt_kv: bfloat16 [8, 5, 2048, 256], P('grp', None, 'seq')
- d_value_weight: bfloat16 [5120, 128], replicated
The draws below stay inside these ranges and needn't reach their ends.
Inputs may be any that keep to these rules, and one draw needn't show every extreme that they name: `prompt_blocks`: the prompts of a group fill 136 of its 160 block slots; one prompt of each group has 32 blocks. `response_order`: each group's row is a permutation. `response_len`: each group's lengths sum to 2457; one response of each group has 64.
All inputs are finite; a program needn't handle non-finite values.
Results may differ from the reference program's by a relative error of at most 0.019.
Values may be sent and summed in bfloat16 or wider, within the bound.
No kernel may reach another device: no remote copies, remote signals or barrier semaphores. Data moves between devices by JAX's collectives and lax.ppermute only.
A program may use at most 128 MiB of HBM per device.

```python
import math
import jax
import jax.numpy as jnp
import numpy as np
from jax import lax

D = 5120
HD = 128
HEADS = 5
RLEN = 64
RPP = 8
PB = 64
GRPS = 8
RESPONSES = 64
PROMPTS = 8
TOKENS = 4096
MAXB = 32
PBLK_DEV = 5
SLOTS = 160
TOTAL_BLOCKS = 136
LIVE = 2457
KEYS_ALL = 114688
N_SEQ = 32


def common_keys(key):
    return jnp.clip(jax.random.normal(key, (GRPS, TOKENS, HD), jnp.float32), -5.0, 5.0)


def draw_queries(key, part):
    key = jax.random.fold_in(key, 11)
    result = jnp.clip(jax.random.normal(key, (GRPS, TOKENS, HEADS, HD), jnp.float32), -5.0, 5.0)
    return result.reshape(GRPS, TOKENS, HEADS * HD).astype(jnp.bfloat16)


def draw_resp_kv(key, part):
    base = common_keys(key)
    key = jax.random.fold_in(key, 12)
    value_key = jax.random.fold_in(key, 0)
    value_rows = jnp.clip(jax.random.normal(value_key, (GRPS, TOKENS, HD), jnp.float32), -5.0, 5.0)
    key_rows = base
    return jnp.concatenate([key_rows, value_rows], axis=2).astype(jnp.bfloat16)


def level_of(own_key, dims, shards, least, largest):
    level = 1.0
    for dim, shards_of in shards:
        draws = jax.random.uniform(jax.random.fold_in(jax.random.fold_in(own_key, 6), dim), (shards_of,), jnp.float32, least / len(shards), largest / len(shards))
        level = level * jnp.repeat(jnp.exp(draws), dims[dim] // shards_of).reshape((-1,) + (1,) * (len(dims) - 1 - dim))
    return level


def length_profile(count, total, most, slope):
    weights = [(1 << 20) // math.isqrt(grade ** slope) + 1 for grade in range(2, count + 1)]
    spare, holding = total - most - (count - 1), [1] * (count - 1)
    while spare > 0:
        free = [i for i in range(count - 1) if holding[i] < most]
        whole, left = sum([weights[i] for i in free]), spare
        for i in free:
            more = min(most - holding[i], max(1, left * weights[i] // whole), spare)
            holding[i] = holding[i] + more
            spare = spare - more
    return np.array([most] + holding)


def uneven_parts(stream_key, count, total, most, slope):
    if count == 2:
        one = jax.random.randint(stream_key, (), max(1, total - most), min(most, total - 1) + 1)
        return jnp.stack([one, total - one])
    lengths = jnp.asarray(length_profile(count, total, most, slope), jnp.int32)
    pairs = (count - 1) // 2
    giver, taker = lengths[1:1 + 2 * pairs:2], lengths[2:2 + 2 * pairs:2]
    room = jnp.minimum(giver - 1, most - taker)
    passed = jax.random.randint(jax.random.fold_in(stream_key, 1), (pairs,), 0, 1 << 20) % (room + 1)
    lengths = lengths.at[1:1 + 2 * pairs:2].set(giver - passed).at[2:2 + 2 * pairs:2].set(taker + passed)
    return lengths[jax.random.permutation(jax.random.fold_in(stream_key, 2), count)]


def normal_values(key, dims, deviation, limit, cuts=(), held_as=jnp.bfloat16):
    values = deviation * jax.random.normal(key, dims, jnp.float32)
    if cuts:
        values = values * level_of(key, dims, cuts, -0.22, 0.18)
    return jnp.clip(values, -limit, limit).astype(held_as)


def setup_inputs(seed: int = 0) -> dict:
    seeds = jax.random.split(jax.random.key(seed), 10)
    return {
        "queries": draw_queries(jax.random.fold_in(seeds[9], 71), 0),
        "resp_kv": draw_resp_kv(jax.random.fold_in(seeds[9], 71), 0),
        "grad_out": normal_values(seeds[2], (GRPS, TOKENS, HEADS * HD), 1.0, 6.0, ((0, 8), (1, 32))),
        "prompt_kv": normal_values(seeds[3], (GRPS, PBLK_DEV, N_SEQ * PB, 2 * HD), 1.0, 5.0, ((0, 8), (2, 32))),
        "resp_inputs": normal_values(seeds[4], (GRPS, TOKENS, D), 1.0, 6.0, ((0, 8), (1, 32))),
        "prompt_inputs": normal_values(seeds[5], (GRPS, PBLK_DEV, N_SEQ * PB, D), 1.0, 6.0, ((0, 8), (2, 32))),
        "prompt_blocks": jax.vmap(lambda own: uneven_parts(own, PROMPTS, TOTAL_BLOCKS, MAXB, 2))(jax.random.split(seeds[6], GRPS)).reshape((GRPS, PROMPTS)).astype(jnp.int32),
        "response_order": jax.vmap(lambda own: jax.random.permutation(own, RESPONSES))(jax.random.split(seeds[7], GRPS)).reshape((GRPS, RESPONSES)).astype(jnp.int32),
        "response_len": jax.vmap(lambda own: uneven_parts(own, RESPONSES, LIVE, RLEN, 1))(jax.random.split(seeds[8], GRPS)).reshape((GRPS, RESPONSES)).astype(jnp.int32),
    }


def response_grads(query_rows, key_values, live_grad, allowed):
    scaling = HD ** -0.5
    query_heads = query_rows.reshape(query_rows.shape[0], HEADS, HD).astype(jnp.float32)
    grad_heads = live_grad.reshape(live_grad.shape[0], HEADS, HD).astype(jnp.float32)
    key_rows = key_values[:, :HD].astype(jnp.float32)
    value_rows = key_values[:, HD:].astype(jnp.float32)
    scores = jnp.einsum("qhd,kd->hqk", query_heads, key_rows) * scaling
    scores = jnp.where(allowed[None], scores, -1e30)
    row_max = jnp.max(scores, axis=-1, keepdims=True)
    raised = jnp.exp(scores - row_max)
    prob_rows = raised / jnp.sum(raised, axis=-1, keepdims=True)
    prob_half = prob_rows.astype(jnp.bfloat16).astype(jnp.float32)
    prob_grad = jnp.einsum("qhd,kd->hqk", grad_heads, value_rows)
    row_total = jnp.sum(prob_rows * prob_grad, axis=-1, keepdims=True)
    score_grad = (prob_rows * (prob_grad - row_total)).astype(jnp.bfloat16).astype(jnp.float32)
    query_grad = jnp.einsum("hqk,kd->qhd", score_grad, key_rows) * scaling
    key_grad = jnp.einsum("hqk,qhd->kd", score_grad, query_heads) * scaling
    value_grad = jnp.einsum("hqk,qhd->kd", prob_half, grad_heads)
    query_grad = query_grad.reshape(query_rows.shape[0], HEADS * HD).astype(jnp.bfloat16)
    return query_grad, jnp.concatenate([key_grad, value_grad], axis=1)


def reference(queries, resp_kv, grad_out, prompt_kv, resp_inputs, prompt_inputs, prompt_blocks, response_order, response_len):
    slot_kv = prompt_kv.reshape(GRPS, SLOTS, PB, 2 * HD)
    starts = (jnp.cumsum(prompt_blocks, axis=1) - prompt_blocks).astype(jnp.int32)
    prompt_of = (response_order // RPP).astype(jnp.int32)
    begin_slot = jnp.take_along_axis(starts, prompt_of, axis=1).reshape(-1).astype(jnp.int32)
    block_count = jnp.take_along_axis(prompt_blocks, prompt_of, axis=1).reshape(-1).astype(jnp.int32)
    query_flat = queries.reshape(GRPS * RESPONSES, RLEN, HEADS * HD)
    kv_flat = resp_kv.reshape(GRPS * RESPONSES, RLEN, 2 * HD)
    grad_flat = grad_out.reshape(GRPS * RESPONSES, RLEN, HEADS * HD)
    live_lengths = response_len.reshape(-1).astype(jnp.int32)
    row_ids = jnp.arange(RLEN, dtype=jnp.int32)
    causal = row_ids[:, None] >= row_ids[None, :]
    block_ids = jnp.arange(MAXB, dtype=jnp.int32)

    def process(slot_total, bundle):
        flat_index, query_rows, kv_rows, grad_rows, first_slot, blocks_here, length = bundle
        group_id = (flat_index // RESPONSES).astype(jnp.int32)
        usable = block_ids < blocks_here
        slot_list = jnp.minimum(first_slot + block_ids, SLOTS - 1).astype(jnp.int32)
        group_kv = lax.dynamic_index_in_dim(slot_kv, group_id, 0, keepdims=False)
        fetched = jnp.take(group_kv, slot_list, axis=0).reshape(MAXB * PB, 2 * HD)
        prompt_seen = jnp.repeat(usable, PB)
        allowed = jnp.concatenate([jnp.broadcast_to(prompt_seen[None, :], (RLEN, MAXB * PB)), causal], axis=1)
        live_rows = row_ids < length
        live_grad = jnp.where(live_rows[:, None], grad_rows, jnp.zeros_like(grad_rows))
        query_grad, kv_grads = response_grads(query_rows, jnp.concatenate([fetched, kv_rows], axis=0), live_grad, allowed)
        prompt_part = kv_grads[:MAXB * PB].reshape(MAXB, PB, 2 * HD)
        prompt_part = jnp.where(usable[:, None, None], prompt_part, jnp.zeros_like(prompt_part))
        slot_total = slot_total.at[group_id, slot_list].add(prompt_part)
        return slot_total, (query_grad, kv_grads[MAXB * PB:].astype(jnp.bfloat16))

    initial = jnp.zeros((GRPS, SLOTS, PB, 2 * HD), jnp.float32)
    indices = jnp.arange(GRPS * RESPONSES, dtype=jnp.int32)
    slot_total, (query_grads, resp_grads) = lax.scan(process, initial, (indices, query_flat, kv_flat, grad_flat, begin_slot, block_count, live_lengths))
    d_queries = query_grads.reshape(GRPS, TOKENS, HEADS * HD)
    d_resp_kv = resp_grads.reshape(GRPS, TOKENS, 2 * HD)
    d_prompt_kv = slot_total.astype(jnp.bfloat16).reshape(GRPS, PBLK_DEV, N_SEQ * PB, 2 * HD)
    weight_term = jnp.dot(resp_inputs.reshape(-1, D).T, d_resp_kv[:, :, HD:].reshape(-1, HD), preferred_element_type=jnp.float32)
    weight_term = weight_term + jnp.dot(prompt_inputs.reshape(-1, D).T, d_prompt_kv[..., HD:].reshape(-1, HD), preferred_element_type=jnp.float32)
    d_value_weight = (weight_term * (KEYS_ALL ** -0.5)).astype(jnp.bfloat16)
    return d_queries, d_resp_kv, d_prompt_kv, d_value_weight
```

```python
import functools

import jax
import jax.numpy as jnp
from jax import lax
from jax.experimental import pallas as pl
from jax.experimental.pallas import tpu as pltpu
from jax.sharding import PartitionSpec as P

HD = 128
HEADS = 5
RLEN = 64
RESP_DEV = 2
RPP = 8
PB = 64
ROWS = HEADS * RLEN
SCALING = HD ** (-0.5)
LOG2E = 1.4426950408889634
OWN_BLOCKS = 4
NT = (((1,), (1,)), ((), ()))
TN = (((0,), (0,)), ((), ()))


def first_block(blocks_ref, prompt):
    total = jnp.int32(0)
    for i in range(blocks_ref.shape[0]):
        total = total + jnp.where(i < prompt, blocks_ref[i], 0)
    return total


def fill_starts(blocks_ref, starts_ref):
    total = jnp.int32(0)
    for i in range(blocks_ref.shape[0]):
        starts_ref[i] = total
        total = total + blocks_ref[i]


def place_of(response, owner, order_ref, starts_ref, owners, slot_rows):
    begin = starts_ref[order_ref[response] >> 3]
    offset = (owner - begin) & (owners - 1)
    return jnp.minimum((begin + offset) >> (owners.bit_length() - 1), slot_rows - 1)


def pack_kernel(owners, pos_ref, blocks_ref, order_ref, kv_ref, out_ref, starts_ref):
    fill_starts(blocks_ref, starts_ref)
    owner = pos_ref[0]

    def body(response, carry):
        place = place_of(response, owner, order_ref, starts_ref, owners, kv_ref.shape[0])
        out_ref[response] = kv_ref[place]
        return carry

    lax.fori_loop(0, out_ref.shape[0], body, 0)


def attention_kernel(
    owners,
    pos_ref,
    blocks_ref,
    order_ref,
    len_ref,
    query_ref,
    own_ref,
    grad_ref,
    got_ref,
    dq_ref,
    down_ref,
    back_ref,
    score_ref,
    pgrad_ref,
):
    f32, bf16 = jnp.float32, jnp.bfloat16
    chunk = OWN_BLOCKS * PB
    chunks = owners // OWN_BLOCKS
    factor = SCALING * LOG2E
    for member in range(RESP_DEV):
        prompt = order_ref[pos_ref[0] * RESP_DEV + member] >> 3
        begin = first_block(blocks_ref, prompt)
        count = blocks_ref[prompt]
        rows = slice(member * RLEN, (member + 1) * RLEN)
        q = jnp.concatenate(
            [query_ref[rows, h * HD : (h + 1) * HD] for h in range(HEADS)], axis=0
        )
        g = jnp.concatenate([grad_ref[rows, h * HD : (h + 1) * HD] for h in range(HEADS)], axis=0)
        row_ids = lax.broadcasted_iota(jnp.int32, (ROWS, HD), 0) & (RLEN - 1)
        g = jnp.where(row_ids < len_ref[member], g, jnp.zeros_like(g))

        def keys_of(i):
            if i < chunks:
                part = got_ref[i * OWN_BLOCKS : (i + 1) * OWN_BLOCKS, member]
                return part.reshape(chunk, 2 * HD)
            return own_ref[rows, :]

        def rows_of(i):
            return slice(i * chunk, i * chunk + (chunk if i < chunks else RLEN))

        top = jnp.full((8, ROWS), -1e30, f32)
        for i in range(chunks + 1):
            kv = keys_of(i)
            s = lax.dot_general(kv[:, :HD], q, NT, preferred_element_type=f32)
            key_ids = lax.broadcasted_iota(jnp.int32, s.shape, 0)
            if i < chunks:
                offset = ((key_ids >> 6) + (i * OWN_BLOCKS - begin)) & (owners - 1)
                s = jnp.where(offset < count, s, -1e30)
            else:
                query_ids = lax.broadcasted_iota(jnp.int32, s.shape, 1) & (RLEN - 1)
                s = jnp.where(key_ids <= query_ids, s, -1e30)
            score_ref[rows_of(i), :] = s
            top = jnp.maximum(top, jnp.max(s.reshape(-1, 8, ROWS), axis=0))
        top = jnp.max(top, axis=0, keepdims=True)
        total = jnp.zeros((8, ROWS), f32)
        mixed = jnp.zeros((8, ROWS), f32)
        for i in range(chunks + 1):
            kv = keys_of(i)
            pg = lax.dot_general(kv[:, HD:], g, NT, preferred_element_type=f32)
            e = jnp.exp2((score_ref[rows_of(i), :] - top) * factor)
            score_ref[rows_of(i), :] = e
            pgrad_ref[rows_of(i), :] = pg
            total = total + jnp.sum(e.reshape(-1, 8, ROWS), axis=0)
            mixed = mixed + jnp.sum((e * pg).reshape(-1, 8, ROWS), axis=0)
        inverse = 1.0 / jnp.sum(total, axis=0, keepdims=True)
        row_total = jnp.sum(mixed, axis=0, keepdims=True) * inverse
        dqt = jnp.zeros((HD, ROWS), f32)
        for i in range(chunks + 1):
            kv = keys_of(i)
            p = score_ref[rows_of(i), :] * inverse
            ds = (p * (pgrad_ref[rows_of(i), :] - row_total)).astype(bf16)
            dk = lax.dot_general(ds, q, (((1,), (0,)), ((), ())), preferred_element_type=f32)
            dv = lax.dot_general(
                p.astype(bf16), g, (((1,), (0,)), ((), ())), preferred_element_type=f32
            )
            dkv = jnp.concatenate([dk * SCALING, dv], axis=1).astype(bf16)
            if i < chunks:
                back_ref[i * OWN_BLOCKS : (i + 1) * OWN_BLOCKS, member] = dkv.reshape(
                    OWN_BLOCKS, PB, 2 * HD
                )
            else:
                down_ref[rows, :] = dkv
            dqt = dqt + lax.dot_general(kv[:, :HD], ds, TN, preferred_element_type=f32)
        dq = (dqt * SCALING).T.astype(bf16)
        for h in range(HEADS):
            dq_ref[rows, h * HD : (h + 1) * HD] = dq[h * RLEN : (h + 1) * RLEN]


def combine_kernel(owners, pos_ref, blocks_ref, order_ref, got_ref, out_ref, starts_ref, acc_ref):
    fill_starts(blocks_ref, starts_ref)
    owner = pos_ref[0]
    acc_ref[...] = jnp.zeros_like(acc_ref)

    def body(response, carry):
        place = place_of(response, owner, order_ref, starts_ref, owners, out_ref.shape[0])
        acc_ref[place] += got_ref[response].astype(jnp.float32)
        return carry

    lax.fori_loop(0, got_ref.shape[0], body, 0)
    out_ref[...] = acc_ref[...].astype(jnp.bfloat16)


def smem():
    return pl.BlockSpec(memory_space=pltpu.SMEM)


def vmem():
    return pl.BlockSpec(memory_space=pltpu.VMEM)


def params():
    return pltpu.CompilerParams(vmem_limit_bytes=40 * 1024 * 1024)


def grp_sum(part, grp_count):
    own = part.astype(jnp.bfloat16)
    step = 1
    total = part
    while step < grp_count:
        width = min(4, grp_count // step)
        total = own.astype(jnp.float32)
        for k in range(1, width):
            pairs = [(i, i ^ (k * step)) for i in range(grp_count)]
            total = total + lax.ppermute(own, "grp", pairs).astype(jnp.float32)
        own = total.astype(jnp.bfloat16)
        step = step * width
    return total


def local(
    queries,
    resp_kv,
    grad_out,
    prompt_kv,
    resp_inputs,
    prompt_inputs,
    prompt_blocks,
    response_order,
    response_len,
):
    bf16, f32 = jnp.bfloat16, jnp.float32
    owners = lax.axis_size("seq")
    grp_count = lax.axis_size("grp")
    slot_rows = prompt_kv.shape[1]
    responses = owners * RESP_DEV
    pos = lax.axis_index("seq").astype(jnp.int32).reshape(1)
    blocks, order, lengths = prompt_blocks[0], response_order[0], response_len[0]

    packed = pl.pallas_call(
        functools.partial(pack_kernel, owners),
        out_shape=jax.ShapeDtypeStruct((responses, PB, 2 * HD), bf16),
        in_specs=[smem(), smem(), smem(), vmem()],
        out_specs=vmem(),
        scratch_shapes=[pltpu.SMEM((blocks.shape[0],), jnp.int32)],
        compiler_params=params(),
        name="pack",
    )(pos, blocks, order, prompt_kv[0])
    fetched = lax.all_to_all(
        packed.reshape(responses * PB, 2 * HD), "seq", 0, 0, tiled=True
    ).reshape(owners, RESP_DEV, PB, 2 * HD)

    keys = owners * PB + RLEN
    d_queries, d_resp_kv, partials = pl.pallas_call(
        functools.partial(attention_kernel, owners),
        out_shape=(
            jax.ShapeDtypeStruct((RESP_DEV * RLEN, HEADS * HD), bf16),
            jax.ShapeDtypeStruct((RESP_DEV * RLEN, 2 * HD), bf16),
            jax.ShapeDtypeStruct((owners, RESP_DEV, PB, 2 * HD), bf16),
        ),
        in_specs=[smem()] * 4 + [vmem()] * 4,
        out_specs=[vmem()] * 3,
        scratch_shapes=[pltpu.VMEM((keys, ROWS), f32), pltpu.VMEM((keys, ROWS), f32)],
        compiler_params=params(),
        name="attention",
    )(pos, blocks, order, lengths, queries[0], resp_kv[0], grad_out[0], fetched)
    returned = lax.all_to_all(
        partials.reshape(responses * PB, 2 * HD), "seq", 0, 0, tiled=True
    ).reshape(responses, PB, 2 * HD)

    d_prompt = pl.pallas_call(
        functools.partial(combine_kernel, owners),
        out_shape=jax.ShapeDtypeStruct((slot_rows, PB, 2 * HD), bf16),
        in_specs=[smem(), smem(), smem(), vmem()],
        out_specs=vmem(),
        scratch_shapes=[
            pltpu.SMEM((blocks.shape[0],), jnp.int32),
            pltpu.VMEM((slot_rows, PB, 2 * HD), f32),
        ],
        compiler_params=params(),
        name="combine",
    )(pos, blocks, order, returned)

    weight_term = jnp.einsum(
        "td,tk->dk", resp_inputs[0], d_resp_kv[:, HD:], preferred_element_type=f32
    ) + jnp.einsum("std,stk->dk", prompt_inputs[0], d_prompt[:, :, HD:], preferred_element_type=f32)
    width = weight_term.shape[0]
    shares = lax.all_to_all(weight_term.astype(bf16), "seq", 0, 0, tiled=True)
    share = jnp.sum(shares.reshape(owners, width // owners, HD).astype(f32), axis=0)
    key_total = grp_count * owners * (RESP_DEV * RLEN + slot_rows * PB)
    share = (grp_sum(share, grp_count) * key_total ** (-0.5)).astype(bf16)
    copies = jnp.broadcast_to(share[None], (owners,) + share.shape)
    d_value_weight = lax.all_to_all(copies.reshape(width, HD), "seq", 0, 0, tiled=True)
    return (d_queries[None], d_resp_kv[None], d_prompt[None], d_value_weight)


def solution(mesh):
    in_specs = (
        P("grp", "seq", None),
        P("grp", "seq", None),
        P("grp", "seq", None),
        P("grp", None, "seq", None),
        P("grp", "seq", None),
        P("grp", None, "seq", None),
        P("grp", None),
        P("grp", None),
        P("grp", "seq"),
    )
    out_specs = (P("grp", "seq", None), P("grp", "seq", None), P("grp", None, "seq", None), P())
    return jax.shard_map(local, mesh=mesh, in_specs=in_specs, out_specs=out_specs, check_vma=False)
```

```python
import functools

import jax
import jax.numpy as jnp
from jax import lax
from jax.experimental import pallas as pl
from jax.experimental.pallas import tpu as pltpu
from jax.sharding import PartitionSpec as P

HD = 128
HEADS = 5
RLEN = 64
RESP_DEV = 2
RPP = 8
PB = 64
ROWS = HEADS * RLEN
SCALING = HD ** (-0.5)
LOG2E = 1.4426950408889634
OWN_BLOCKS = 4
CHUNK = 640
NN = (((1,), (0,)), ((), ()))
NT = (((1,), (1,)), ((), ()))
TN = (((0,), (0,)), ((), ()))


def first_block(blocks_ref, prompt):
    total = jnp.int32(0)
    for i in range(blocks_ref.shape[0]):
        total = total + jnp.where(i < prompt, blocks_ref[i], 0)
    return total


def fill_starts(blocks_ref, starts_ref):
    total = jnp.int32(0)
    for i in range(blocks_ref.shape[0]):
        starts_ref[i] = total
        total = total + blocks_ref[i]


def place_of(response, owner, order_ref, starts_ref, owners, slot_rows):
    begin = starts_ref[order_ref[response] >> 3]
    offset = (owner - begin) & (owners - 1)
    return jnp.minimum((begin + offset) >> (owners.bit_length() - 1), slot_rows - 1)


def pack_kernel(
    owners,
    pos_ref,
    blocks_hbm,
    order_hbm,
    kv_hbm,
    out_ref,
    blocks_ref,
    order_ref,
    starts_ref,
    kv_ref,
    sems,
):
    copies = [
        pltpu.make_async_copy(blocks_hbm.at[0], blocks_ref, sems.at[0]),
        pltpu.make_async_copy(order_hbm.at[0], order_ref, sems.at[1]),
        pltpu.make_async_copy(kv_hbm.at[0], kv_ref, sems.at[2]),
    ]
    for copy in copies:
        copy.start()
    for copy in copies:
        copy.wait()
    fill_starts(blocks_ref, starts_ref)
    owner = pos_ref[0]

    def body(response, carry):
        place = place_of(response, owner, order_ref, starts_ref, owners, kv_ref.shape[0])
        out_ref[response] = kv_ref[place]
        return carry

    lax.fori_loop(0, out_ref.shape[0], body, 0, unroll=8)


def stacked_heads(ref, rows):
    return jnp.concatenate([ref[rows, h * HD : (h + 1) * HD] for h in range(HEADS)], axis=0)


def attention_kernel(
    owners,
    pos_ref,
    blocks_ref,
    order_ref,
    len_ref,
    query_ref,
    own_ref,
    grad_ref,
    got_ref,
    down_v_ref,
    back_v_ref,
    sgrad_hbm,
    score_ref,
    pgrad_ref,
    sgrad_ref,
    sems,
):
    f32, bf16 = jnp.float32, jnp.bfloat16
    chunk = OWN_BLOCKS * PB
    chunks = owners // OWN_BLOCKS
    factor = SCALING * LOG2E
    for member in range(RESP_DEV):
        prompt = order_ref[pos_ref[0] * RESP_DEV + member] >> 3
        begin = first_block(blocks_ref, prompt)
        count = blocks_ref[prompt]
        rows = slice(member * RLEN, (member + 1) * RLEN)
        q = stacked_heads(query_ref, rows)
        g = stacked_heads(grad_ref, rows)
        row_ids = lax.broadcasted_iota(jnp.int32, (ROWS, HD), 0) & (RLEN - 1)
        g = jnp.where(row_ids < len_ref[member], g, jnp.zeros_like(g))

        def part_of(i):
            return slice(i * OWN_BLOCKS, (i + 1) * OWN_BLOCKS)

        def rows_of(i):
            return slice(i * chunk, i * chunk + (chunk if i < chunks else RLEN))

        top = jnp.full((8, ROWS), -1e30, f32)
        for i in range(chunks + 1):
            if i < chunks:
                k = got_ref[part_of(i), member, :, :HD].reshape(chunk, HD)
            else:
                k = own_ref[rows, :HD]
            s = lax.dot_general(k, q, NT, preferred_element_type=f32)
            key_ids = lax.broadcasted_iota(jnp.int32, s.shape, 0)
            if i < chunks:
                offset = ((key_ids >> 6) + (i * OWN_BLOCKS - begin)) & (owners - 1)
                s = jnp.where(offset < count, s, -1e30)
            else:
                query_ids = lax.broadcasted_iota(jnp.int32, s.shape, 1) & (RLEN - 1)
                s = jnp.where(key_ids <= query_ids, s, -1e30)
            score_ref[rows_of(i), :] = s
            top = jnp.maximum(top, jnp.max(s.reshape(-1, 8, ROWS), axis=0))
        top = jnp.max(top, axis=0, keepdims=True)
        total = jnp.zeros((8, ROWS), f32)
        mixed = jnp.zeros((8, ROWS), f32)
        for i in range(chunks + 1):
            if i < chunks:
                v = got_ref[part_of(i), member, :, HD:].reshape(chunk, HD)
            else:
                v = own_ref[rows, HD:]
            pg = lax.dot_general(v, g, NT, preferred_element_type=f32)
            e = jnp.exp2((score_ref[rows_of(i), :] - top) * factor)
            score_ref[rows_of(i), :] = e
            pgrad_ref[rows_of(i), :] = pg
            total = total + jnp.sum(e.reshape(-1, 8, ROWS), axis=0)
            mixed = mixed + jnp.sum((e * pg).reshape(-1, 8, ROWS), axis=0)
        inverse = 1.0 / jnp.sum(total, axis=0, keepdims=True)
        row_total = jnp.sum(mixed, axis=0, keepdims=True) * inverse
        for i in range(chunks + 1):
            p = score_ref[rows_of(i), :] * inverse
            sgrad_ref[member, rows_of(i), :] = (
                p * (pgrad_ref[rows_of(i), :] - row_total)
            ).astype(bf16)
            dv = lax.dot_general(p.astype(bf16), g, NN, preferred_element_type=f32).astype(bf16)
            if i < chunks:
                back_v_ref[part_of(i), member] = dv.reshape(OWN_BLOCKS, PB, HD)
            else:
                down_v_ref[rows, :] = dv
        pltpu.make_async_copy(sgrad_ref.at[member], sgrad_hbm.at[member], sems.at[member]).start()
    for member in range(RESP_DEV):
        pltpu.make_async_copy(sgrad_ref.at[member], sgrad_hbm.at[member], sems.at[member]).wait()


def query_key_kernel(
    owners,
    query_ref,
    own_ref,
    got_ref,
    sgrad_hbm,
    down_v_ref,
    dq_ref,
    down_ref,
    back_k_ref,
    sgrad_ref,
    sems,
):
    copies = [
        pltpu.make_async_copy(sgrad_hbm.at[member], sgrad_ref.at[member], sems.at[member])
        for member in range(RESP_DEV)
    ]
    for copy in copies:
        copy.start()
    f32, bf16 = jnp.float32, jnp.bfloat16
    chunk = OWN_BLOCKS * PB
    chunks = owners // OWN_BLOCKS
    for member in range(RESP_DEV):
        rows = slice(member * RLEN, (member + 1) * RLEN)
        q = stacked_heads(query_ref, rows)
        copies[member].wait()
        dqt = jnp.zeros((HD, ROWS), f32)
        for i in range(chunks + 1):
            part = slice(i * OWN_BLOCKS, (i + 1) * OWN_BLOCKS)
            ds = sgrad_ref[member, i * chunk : i * chunk + (chunk if i < chunks else RLEN), :]
            dk = lax.dot_general(ds, q, NN, preferred_element_type=f32) * SCALING
            if i < chunks:
                k = got_ref[part, member, :, :HD].reshape(chunk, HD)
                back_k_ref[part, member] = dk.astype(bf16).reshape(OWN_BLOCKS, PB, HD)
            else:
                k = own_ref[rows, :HD]
                down_ref[rows, :HD] = dk.astype(bf16)
            dqt = dqt + lax.dot_general(k, ds, TN, preferred_element_type=f32)
        dq = (dqt * SCALING).T.astype(bf16)
        for h in range(HEADS):
            dq_ref[rows, h * HD : (h + 1) * HD] = dq[h * RLEN : (h + 1) * RLEN]
    down_ref[:, HD:] = down_v_ref[...]


def half_weights(resp_in_ref, resp_grad_ref, prompt_in_ref, prompt_grad):
    f32 = jnp.float32
    term = lax.dot_general(resp_in_ref[...], resp_grad_ref[...], TN, preferred_element_type=f32)
    more = lax.dot_general(prompt_in_ref[...], prompt_grad, TN, preferred_element_type=f32)
    return (term + more).astype(jnp.bfloat16)


def sum_blocks(owners, pos_ref, blocks_ref, order_ref, got_ref, starts_ref, acc_ref):
    fill_starts(blocks_ref, starts_ref)
    owner = pos_ref[0]
    acc_ref[...] = jnp.zeros_like(acc_ref)

    def body(response, carry):
        place = place_of(response, owner, order_ref, starts_ref, owners, acc_ref.shape[0])
        acc_ref[place] += got_ref[response].astype(jnp.float32)
        return carry

    lax.fori_loop(0, got_ref.shape[0], body, 0, unroll=8)


def combine_kernel(
    owners,
    pos_ref,
    blocks_ref,
    order_ref,
    got_ref,
    resp_in_ref,
    resp_grad_ref,
    prompt_in_ref,
    out_ref,
    weight_ref,
    starts_ref,
    acc_ref,
):
    @pl.when(pl.program_id(0) == 0)
    def _():
        sum_blocks(owners, pos_ref, blocks_ref, order_ref, got_ref, starts_ref, acc_ref)
        out_ref[...] = acc_ref[...].reshape(out_ref.shape).astype(jnp.bfloat16)

    weight_ref[...] = half_weights(resp_in_ref, resp_grad_ref, prompt_in_ref, out_ref[...])


def join_kernel(
    owners, pos_ref, blocks_ref, order_ref, got_ref, value_ref, out_ref, starts_ref, acc_ref
):
    sum_blocks(owners, pos_ref, blocks_ref, order_ref, got_ref, starts_ref, acc_ref)
    out_ref[:, :HD] = acc_ref[...].reshape(value_ref.shape).astype(jnp.bfloat16)
    out_ref[:, HD:] = value_ref[...]


def weight_kernel(
    pos_ref, resp_in_ref, resp_grad_ref, prompt_in_ref, prompt_grad_ref, weight_ref
):
    weight_ref[...] = half_weights(
        resp_in_ref, resp_grad_ref, prompt_in_ref, prompt_grad_ref[...]
    )


def finish_kernel(pos_ref, mine_ref, theirs_ref, out_hbm, sems):
    half = mine_ref.shape[0]
    core = pos_ref[0] & 1
    copies = [
        pltpu.make_async_copy(
            source, out_hbm.at[pl.ds(pl.multiple_of(place * half, half), half)], sems.at[i]
        )
        for i, (source, place) in enumerate(((mine_ref, core), (theirs_ref, 1 - core)))
    ]
    for copy in copies:
        copy.start()
    for copy in copies:
        copy.wait()


def smem():
    return pl.BlockSpec(memory_space=pltpu.SMEM)


def vmem():
    return pl.BlockSpec(memory_space=pltpu.VMEM)


def hbm():
    return pl.BlockSpec(memory_space=pltpu.HBM)


def in_hbm(x):
    return pltpu.with_memory_space_constraint(x, pltpu.HBM)


def params():
    return pltpu.CompilerParams(vmem_limit_bytes=20 * 1024 * 1024)


def grp_sum(part, grp_count):
    total, step = part, 1
    while step < grp_count:
        width = min(4, grp_count // step)
        own = total.astype(jnp.bfloat16)
        terms = [own.astype(jnp.float32)]
        for k in range(1, width):
            pairs = [(i, i ^ (k * step)) for i in range(grp_count)]
            terms.append(lax.ppermute(own, "grp", pairs).astype(jnp.float32))
        while len(terms) > 1:
            terms = [terms[i] + terms[i + 1] for i in range(0, len(terms), 2)]
        total, step = terms[0], step * width
    return total


def local(
    queries,
    resp_kv,
    grad_out,
    prompt_kv,
    resp_inputs,
    prompt_inputs,
    prompt_blocks,
    response_order,
    response_len,
):
    bf16, f32 = jnp.bfloat16, jnp.float32
    owners = lax.axis_size("seq")
    grp_count = lax.axis_size("grp")
    slot_rows = prompt_kv.shape[1]
    responses = owners * RESP_DEV
    pos = lax.axis_index("seq").astype(jnp.int32).reshape(1)
    blocks, order, lengths = prompt_blocks[0], response_order[0], response_len[0]

    packed = pl.pallas_call(
        functools.partial(pack_kernel, owners),
        out_shape=jax.ShapeDtypeStruct((responses, PB, 2 * HD), bf16),
        in_specs=[smem()] + [hbm()] * 3,
        out_specs=vmem(),
        scratch_shapes=[
            pltpu.SMEM(blocks.shape, jnp.int32),
            pltpu.SMEM(order.shape, jnp.int32),
            pltpu.SMEM(blocks.shape, jnp.int32),
            pltpu.VMEM(prompt_kv.shape[1:2] + (PB, 2 * HD), bf16),
            pltpu.SemaphoreType.DMA((3,)),
        ],
        compiler_params=params(),
        name="pack",
    )(pos, in_hbm(prompt_blocks), in_hbm(response_order), in_hbm(prompt_kv))
    fetched = lax.all_to_all(
        packed.reshape(responses * PB, 2 * HD), "seq", 0, 0, tiled=True
    ).reshape(owners, RESP_DEV, PB, 2 * HD)

    keys = owners * PB + RLEN
    part_shape = jax.ShapeDtypeStruct((owners, RESP_DEV, PB, HD), bf16)
    down_v, part_v, score_grad = pl.pallas_call(
        functools.partial(attention_kernel, owners),
        out_shape=(
            jax.ShapeDtypeStruct((RESP_DEV * RLEN, HD), bf16),
            part_shape,
            pltpu.HBM((RESP_DEV, keys, ROWS), bf16),
        ),
        in_specs=[smem()] * 4 + [vmem()] * 4,
        out_specs=[vmem(), vmem(), hbm()],
        scratch_shapes=[
            pltpu.VMEM((keys, ROWS), f32),
            pltpu.VMEM((keys, ROWS), f32),
            pltpu.VMEM((RESP_DEV, keys, ROWS), bf16),
            pltpu.SemaphoreType.DMA((RESP_DEV,)),
        ],
        compiler_params=params(),
        name="attention",
    )(pos, blocks, order, lengths, queries[0], resp_kv[0], grad_out[0], fetched)

    def to_owners(part):
        got = lax.all_to_all(part.reshape(responses * PB, HD), "seq", 0, 0, tiled=True)
        return got.reshape(responses, PB, HD)

    returned_v = to_owners(part_v)
    d_queries, d_resp_kv, part_k = pl.pallas_call(
        functools.partial(query_key_kernel, owners),
        out_shape=(
            jax.ShapeDtypeStruct((RESP_DEV * RLEN, HEADS * HD), bf16),
            jax.ShapeDtypeStruct((RESP_DEV * RLEN, 2 * HD), bf16),
            part_shape,
        ),
        in_specs=[vmem(), vmem(), vmem(), hbm(), vmem()],
        out_specs=[vmem()] * 3,
        scratch_shapes=[
            pltpu.VMEM((RESP_DEV, keys, ROWS), bf16),
            pltpu.SemaphoreType.DMA((RESP_DEV,)),
        ],
        compiler_params=params(),
        name="query_key",
    )(queries[0], resp_kv[0], fetched, in_hbm(score_grad), down_v)

    rows, prompt_rows = RESP_DEV * RLEN, slot_rows * PB
    width = resp_inputs.shape[2]
    half = width // 2
    steps = half // CHUNK
    resp_in = resp_inputs[0]
    prompt_in = prompt_inputs[0].reshape(prompt_rows, width)

    d_value, sent = pl.pallas_call(
        functools.partial(combine_kernel, owners),
        out_shape=(
            jax.ShapeDtypeStruct((prompt_rows, HD), bf16),
            jax.ShapeDtypeStruct((half, HD), bf16),
        ),
        grid_spec=pltpu.PrefetchScalarGridSpec(
            num_scalar_prefetch=3,
            grid=(steps,),
            in_specs=[
                pl.BlockSpec((responses, PB, HD), lambda i, *_: (0, 0, 0)),
                pl.BlockSpec((rows, CHUNK), lambda i, p, *_: (0, (1 - (p[0] & 1)) * steps + i)),
                pl.BlockSpec((rows, HD), lambda i, *_: (0, 0)),
                pl.BlockSpec(
                    (prompt_rows, CHUNK), lambda i, p, *_: (0, (1 - (p[0] & 1)) * steps + i)
                ),
            ],
            out_specs=[
                pl.BlockSpec((prompt_rows, HD), lambda i, *_: (0, 0)),
                pl.BlockSpec((CHUNK, HD), lambda i, *_: (i, 0)),
            ],
            scratch_shapes=[
                pltpu.SMEM((blocks.shape[0],), jnp.int32),
                pltpu.VMEM((slot_rows, PB, HD), f32),
            ],
        ),
        compiler_params=params(),
        name="combine",
    )(pos, blocks, order, returned_v, resp_in, down_v, prompt_in)
    swap = [(i, i ^ 1) for i in range(owners)]
    from_twin = lax.ppermute(sent, "seq", swap)
    kept = pl.pallas_call(
        weight_kernel,
        out_shape=jax.ShapeDtypeStruct((half, HD), bf16),
        grid_spec=pltpu.PrefetchScalarGridSpec(
            num_scalar_prefetch=1,
            grid=(steps,),
            in_specs=[
                pl.BlockSpec((rows, CHUNK), lambda i, p: (0, (p[0] & 1) * steps + i)),
                pl.BlockSpec((rows, HD), lambda i, p: (0, 0)),
                pl.BlockSpec((prompt_rows, CHUNK), lambda i, p: (0, (p[0] & 1) * steps + i)),
                pl.BlockSpec((prompt_rows, HD), lambda i, p: (0, 0)),
            ],
            out_specs=pl.BlockSpec((CHUNK, HD), lambda i, p: (i, 0)),
        ),
        compiler_params=params(),
        name="weights",
    )(pos, resp_in, down_v, prompt_in, d_value)

    both = (kept.astype(f32) + from_twin.astype(f32)).astype(bf16)
    twins = [list(range(c, owners, 2)) for c in range(2)]
    chips = owners // 2
    shares = lax.all_to_all(both, "seq", 0, 0, tiled=True, axis_index_groups=twins)
    share = jnp.sum(shares.reshape(chips, half // chips, HD).astype(f32), axis=0)
    share, part_k = lax.optimization_barrier((share, part_k))
    returned_k = to_owners(part_k)
    key_total = grp_count * owners * (rows + prompt_rows)
    share = (grp_sum(share, grp_count) * key_total ** (-0.5)).astype(bf16)
    share, returned_k = lax.optimization_barrier((share, returned_k))
    copies = jnp.broadcast_to(share[None], (chips,) + share.shape).reshape(half, HD)
    mine = lax.all_to_all(copies, "seq", 0, 0, tiled=True, axis_index_groups=twins)
    theirs = lax.ppermute(mine, "seq", swap)
    d_value_weight = pl.pallas_call(
        finish_kernel,
        out_shape=pltpu.HBM((width, HD), bf16),
        in_specs=[smem(), vmem(), vmem()],
        out_specs=hbm(),
        scratch_shapes=[pltpu.SemaphoreType.DMA((2,))],
        compiler_params=params(),
        name="finish",
    )(pos, mine, theirs)
    d_prompt = pl.pallas_call(
        functools.partial(join_kernel, owners),
        out_shape=jax.ShapeDtypeStruct((prompt_rows, 2 * HD), bf16),
        in_specs=[smem()] * 3 + [vmem()] * 2,
        out_specs=vmem(),
        scratch_shapes=[
            pltpu.SMEM(blocks.shape, jnp.int32),
            pltpu.VMEM((slot_rows, PB, HD), f32),
        ],
        compiler_params=params(),
        name="join",
    )(pos, blocks, order, returned_k, d_value)
    d_prompt = d_prompt.reshape(slot_rows, PB, 2 * HD)
    return (d_queries[None], d_resp_kv[None], d_prompt[None], d_value_weight)


def solution(mesh):
    in_specs = (
        P("grp", "seq", None),
        P("grp", "seq", None),
        P("grp", "seq", None),
        P("grp", None, "seq", None),
        P("grp", "seq", None),
        P("grp", None, "seq", None),
        P("grp", None),
        P("grp", None),
        P("grp", "seq"),
    )
    out_specs = (P("grp", "seq", None), P("grp", "seq", None), P("grp", None, "seq", None), P())
    return jax.shard_map(local, mesh=mesh, in_specs=in_specs, out_specs=out_specs, check_vma=False)
```

```python
import functools

import jax
import jax.numpy as jnp
from jax import lax
from jax.experimental import pallas as pl
from jax.experimental.pallas import tpu as pltpu
from jax.sharding import PartitionSpec as P

HD = 128
HEADS = 5
RLEN = 64
RESP_DEV = 2
RPP = 8
PB = 64
ROWS = HEADS * RLEN
SCALING = HD ** (-0.5)
LOG2E = 1.4426950408889634
OWN_BLOCKS = 4
CHUNK = 640
NN = (((1,), (0,)), ((), ()))
NT = (((1,), (1,)), ((), ()))
TN = (((0,), (0,)), ((), ()))


def first_block(blocks_ref, prompt):
    total = jnp.int32(0)
    for i in range(blocks_ref.shape[0]):
        total = total + jnp.where(i < prompt, blocks_ref[i], 0)
    return total


def fill_starts(blocks_ref, starts_ref):
    total = jnp.int32(0)
    for i in range(blocks_ref.shape[0]):
        starts_ref[i] = total
        total = total + blocks_ref[i]


def place_of(response, owner, order_ref, starts_ref, owners, slot_rows):
    begin = starts_ref[order_ref[response] >> 3]
    offset = (owner - begin) & (owners - 1)
    return jnp.minimum((begin + offset) >> (owners.bit_length() - 1), slot_rows - 1)


def pack_kernel(
    owners,
    pos_ref,
    blocks_hbm,
    order_hbm,
    kv_hbm,
    out_ref,
    blocks_ref,
    order_ref,
    starts_ref,
    kv_ref,
    sems,
):
    copies = [
        pltpu.make_async_copy(blocks_hbm.at[0], blocks_ref, sems.at[0]),
        pltpu.make_async_copy(order_hbm.at[0], order_ref, sems.at[1]),
        pltpu.make_async_copy(kv_hbm.at[0], kv_ref, sems.at[2]),
    ]
    for copy in copies:
        copy.start()
    for copy in copies:
        copy.wait()
    fill_starts(blocks_ref, starts_ref)
    owner = pos_ref[0]

    def body(response, carry):
        place = place_of(response, owner, order_ref, starts_ref, owners, kv_ref.shape[0])
        out_ref[response] = kv_ref[place]
        return carry

    lax.fori_loop(0, out_ref.shape[0], body, 0, unroll=8)


def stacked_heads(ref, rows):
    return jnp.concatenate([ref[rows, h * HD : (h + 1) * HD] for h in range(HEADS)], axis=0)


def attention_kernel(
    owners,
    pos_ref,
    blocks_ref,
    order_ref,
    len_ref,
    query_ref,
    own_ref,
    grad_ref,
    got_ref,
    down_v_ref,
    back_v_ref,
    sgrad_hbm,
    score_ref,
    pgrad_ref,
    sgrad_ref,
    sems,
):
    f32, bf16 = jnp.float32, jnp.bfloat16
    chunk = OWN_BLOCKS * PB
    chunks = owners // OWN_BLOCKS
    factor = SCALING * LOG2E
    for member in range(RESP_DEV):
        prompt = order_ref[pos_ref[0] * RESP_DEV + member] >> 3
        begin = first_block(blocks_ref, prompt)
        count = blocks_ref[prompt]
        rows = slice(member * RLEN, (member + 1) * RLEN)
        q = stacked_heads(query_ref, rows)
        g = stacked_heads(grad_ref, rows)
        row_ids = lax.broadcasted_iota(jnp.int32, (ROWS, HD), 0) & (RLEN - 1)
        g = jnp.where(row_ids < len_ref[member], g, jnp.zeros_like(g))

        def part_of(i):
            return slice(i * OWN_BLOCKS, (i + 1) * OWN_BLOCKS)

        def rows_of(i):
            return slice(i * chunk, i * chunk + (chunk if i < chunks else RLEN))

        top = jnp.full((8, ROWS), -1e30, f32)
        for i in range(chunks + 1):
            if i < chunks:
                k = got_ref[part_of(i), member, :, :HD].reshape(chunk, HD)
            else:
                k = own_ref[rows, :HD]
            s = lax.dot_general(k, q, NT, preferred_element_type=f32)
            if i < chunks:
                seen = []
                for j in range(OWN_BLOCKS):
                    offset = (i * OWN_BLOCKS + j - begin) & (owners - 1)
                    hidden = jnp.where(offset < count, 0.0, -1e30)
                    seen.append(s[j * PB : (j + 1) * PB] + hidden)
                s = jnp.concatenate(seen, axis=0)
            else:
                key_ids = lax.broadcasted_iota(jnp.int32, s.shape, 0)
                query_ids = lax.broadcasted_iota(jnp.int32, s.shape, 1) & (RLEN - 1)
                s = jnp.where(key_ids <= query_ids, s, -1e30)
            score_ref[rows_of(i), :] = s
            top = jnp.maximum(top, jnp.max(s.reshape(-1, 8, ROWS), axis=0))
        top = jnp.max(top, axis=0, keepdims=True)
        total = jnp.zeros((8, ROWS), f32)
        mixed = jnp.zeros((8, ROWS), f32)
        for i in range(chunks + 1):
            if i < chunks:
                v = got_ref[part_of(i), member, :, HD:].reshape(chunk, HD)
            else:
                v = own_ref[rows, HD:]
            pg = lax.dot_general(v, g, NT, preferred_element_type=f32)
            e = jnp.exp2((score_ref[rows_of(i), :] - top) * factor)
            score_ref[rows_of(i), :] = e
            pgrad_ref[rows_of(i), :] = pg
            total = total + jnp.sum(e.reshape(-1, 8, ROWS), axis=0)
            mixed = mixed + jnp.sum((e * pg).reshape(-1, 8, ROWS), axis=0)
        inverse = 1.0 / jnp.sum(total, axis=0, keepdims=True)
        row_total = jnp.sum(mixed, axis=0, keepdims=True) * inverse
        for i in range(chunks + 1):
            p = score_ref[rows_of(i), :] * inverse
            sgrad_ref[member, rows_of(i), :] = (
                p * (pgrad_ref[rows_of(i), :] - row_total)
            ).astype(bf16)
            dv = lax.dot_general(p.astype(bf16), g, NN, preferred_element_type=f32).astype(bf16)
            if i < chunks:
                back_v_ref[part_of(i), member] = dv.reshape(OWN_BLOCKS, PB, HD)
            else:
                down_v_ref[rows, :] = dv
        pltpu.make_async_copy(sgrad_ref.at[member], sgrad_hbm.at[member], sems.at[member]).start()
    for member in range(RESP_DEV):
        pltpu.make_async_copy(sgrad_ref.at[member], sgrad_hbm.at[member], sems.at[member]).wait()


def query_key_kernel(
    owners,
    query_ref,
    own_ref,
    got_ref,
    sgrad_hbm,
    down_v_ref,
    dq_ref,
    down_ref,
    back_k_ref,
    sgrad_ref,
    sems,
):
    copies = [
        pltpu.make_async_copy(sgrad_hbm.at[member], sgrad_ref.at[member], sems.at[member])
        for member in range(RESP_DEV)
    ]
    for copy in copies:
        copy.start()
    f32, bf16 = jnp.float32, jnp.bfloat16
    chunk = OWN_BLOCKS * PB
    chunks = owners // OWN_BLOCKS
    for member in range(RESP_DEV):
        rows = slice(member * RLEN, (member + 1) * RLEN)
        q = stacked_heads(query_ref, rows)
        copies[member].wait()
        dqt = jnp.zeros((HD, ROWS), f32)
        for i in range(chunks + 1):
            part = slice(i * OWN_BLOCKS, (i + 1) * OWN_BLOCKS)
            ds = sgrad_ref[member, i * chunk : i * chunk + (chunk if i < chunks else RLEN), :]
            dk = lax.dot_general(ds, q, NN, preferred_element_type=f32) * SCALING
            if i < chunks:
                k = got_ref[part, member, :, :HD].reshape(chunk, HD)
                back_k_ref[part, member] = dk.astype(bf16).reshape(OWN_BLOCKS, PB, HD)
            else:
                k = own_ref[rows, :HD]
                down_ref[rows, :HD] = dk.astype(bf16)
            dqt = dqt + lax.dot_general(k, ds, TN, preferred_element_type=f32)
        dq = (dqt * SCALING).T.astype(bf16)
        for h in range(HEADS):
            dq_ref[rows, h * HD : (h + 1) * HD] = dq[h * RLEN : (h + 1) * RLEN]
    down_ref[:, HD:] = down_v_ref[...]


def half_weights(core, resp_in_ref, resp_grad, prompt_in_ref, prompt_grad, weight_ref):
    half = weight_ref.shape[0]
    for i in range(half // CHUNK):
        place = pl.ds(pl.multiple_of(core * half + i * CHUNK, HD), CHUNK)
        term = lax.dot_general(
            resp_in_ref[:, place], resp_grad, TN, preferred_element_type=jnp.float32
        )
        more = lax.dot_general(
            prompt_in_ref[:, place], prompt_grad, TN, preferred_element_type=jnp.float32
        )
        weight_ref[i * CHUNK : (i + 1) * CHUNK, :] = (term + more).astype(jnp.bfloat16)


def sum_blocks(owners, pos_ref, blocks_ref, order_ref, got_ref, starts_ref, acc_ref):
    fill_starts(blocks_ref, starts_ref)
    owner = pos_ref[0]
    acc_ref[...] = jnp.zeros_like(acc_ref)

    def body(response, carry):
        place = place_of(response, owner, order_ref, starts_ref, owners, acc_ref.shape[0])
        acc_ref[place] += got_ref[response].astype(jnp.float32)
        return carry

    lax.fori_loop(0, got_ref.shape[0], body, 0, unroll=8)


def combine_kernel(
    owners,
    pos_ref,
    blocks_ref,
    order_ref,
    got_ref,
    resp_in_ref,
    resp_grad_ref,
    prompt_in_ref,
    out_ref,
    weight_ref,
    starts_ref,
    acc_ref,
):
    sum_blocks(owners, pos_ref, blocks_ref, order_ref, got_ref, starts_ref, acc_ref)
    prompt_grad = acc_ref[...].reshape(out_ref.shape).astype(jnp.bfloat16)
    out_ref[...] = prompt_grad
    other = 1 - (pos_ref[0] & 1)
    half_weights(other, resp_in_ref, resp_grad_ref[...], prompt_in_ref, prompt_grad, weight_ref)


def join_kernel(
    owners, pos_ref, blocks_ref, order_ref, got_ref, value_ref, out_ref, starts_ref, acc_ref
):
    sum_blocks(owners, pos_ref, blocks_ref, order_ref, got_ref, starts_ref, acc_ref)
    out_ref[:, :HD] = acc_ref[...].reshape(value_ref.shape).astype(jnp.bfloat16)
    out_ref[:, HD:] = value_ref[...]


def weight_kernel(
    pos_ref, resp_in_ref, resp_grad_ref, prompt_in_ref, prompt_grad_ref, weight_ref
):
    half_weights(
        pos_ref[0] & 1,
        resp_in_ref,
        resp_grad_ref[...],
        prompt_in_ref,
        prompt_grad_ref[...],
        weight_ref,
    )


def finish_kernel(pos_ref, mine_ref, theirs_ref, out_hbm, sems):
    half = mine_ref.shape[0]
    core = pos_ref[0] & 1
    copies = [
        pltpu.make_async_copy(
            source, out_hbm.at[pl.ds(pl.multiple_of(place * half, half), half)], sems.at[i]
        )
        for i, (source, place) in enumerate(((mine_ref, core), (theirs_ref, 1 - core)))
    ]
    for copy in copies:
        copy.start()
    for copy in copies:
        copy.wait()


def smem():
    return pl.BlockSpec(memory_space=pltpu.SMEM)


def vmem():
    return pl.BlockSpec(memory_space=pltpu.VMEM)


def hbm():
    return pl.BlockSpec(memory_space=pltpu.HBM)


def in_hbm(x):
    return pltpu.with_memory_space_constraint(x, pltpu.HBM)


def params():
    return pltpu.CompilerParams(vmem_limit_bytes=20 * 1024 * 1024)


def grp_sum(part, grp_count):
    total, step = part, 1
    while step < grp_count:
        width = min(4, grp_count // step)
        own = total.astype(jnp.bfloat16)
        terms = [own.astype(jnp.float32)]
        for k in range(1, width):
            pairs = [(i, i ^ (k * step)) for i in range(grp_count)]
            terms.append(lax.ppermute(own, "grp", pairs).astype(jnp.float32))
        while len(terms) > 1:
            terms = [terms[i] + terms[i + 1] for i in range(0, len(terms), 2)]
        total, step = terms[0], step * width
    return total


def local(
    queries,
    resp_kv,
    grad_out,
    prompt_kv,
    resp_inputs,
    prompt_inputs,
    prompt_blocks,
    response_order,
    response_len,
):
    bf16, f32 = jnp.bfloat16, jnp.float32
    owners = lax.axis_size("seq")
    grp_count = lax.axis_size("grp")
    slot_rows = prompt_kv.shape[1]
    responses = owners * RESP_DEV
    pos = lax.axis_index("seq").astype(jnp.int32).reshape(1)
    blocks, order, lengths = prompt_blocks[0], response_order[0], response_len[0]

    packed = pl.pallas_call(
        functools.partial(pack_kernel, owners),
        out_shape=jax.ShapeDtypeStruct((responses, PB, 2 * HD), bf16),
        in_specs=[smem()] + [hbm()] * 3,
        out_specs=vmem(),
        scratch_shapes=[
            pltpu.SMEM(blocks.shape, jnp.int32),
            pltpu.SMEM(order.shape, jnp.int32),
            pltpu.SMEM(blocks.shape, jnp.int32),
            pltpu.VMEM(prompt_kv.shape[1:2] + (PB, 2 * HD), bf16),
            pltpu.SemaphoreType.DMA((3,)),
        ],
        compiler_params=params(),
        name="pack",
    )(pos, in_hbm(prompt_blocks), in_hbm(response_order), in_hbm(prompt_kv))
    fetched = lax.all_to_all(
        packed.reshape(responses * PB, 2 * HD), "seq", 0, 0, tiled=True
    ).reshape(owners, RESP_DEV, PB, 2 * HD)

    keys = owners * PB + RLEN
    part_shape = jax.ShapeDtypeStruct((owners, RESP_DEV, PB, HD), bf16)
    down_v, part_v, score_grad = pl.pallas_call(
        functools.partial(attention_kernel, owners),
        out_shape=(
            jax.ShapeDtypeStruct((RESP_DEV * RLEN, HD), bf16),
            part_shape,
            pltpu.HBM((RESP_DEV, keys, ROWS), bf16),
        ),
        in_specs=[smem()] * 4 + [vmem()] * 4,
        out_specs=[vmem(), vmem(), hbm()],
        scratch_shapes=[
            pltpu.VMEM((keys, ROWS), f32),
            pltpu.VMEM((keys, ROWS), f32),
            pltpu.VMEM((RESP_DEV, keys, ROWS), bf16),
            pltpu.SemaphoreType.DMA((RESP_DEV,)),
        ],
        compiler_params=params(),
        name="attention",
    )(pos, blocks, order, lengths, queries[0], resp_kv[0], grad_out[0], fetched)

    def to_owners(part):
        got = lax.all_to_all(part.reshape(responses * PB, HD), "seq", 0, 0, tiled=True)
        return got.reshape(responses, PB, HD)

    returned_v = to_owners(part_v)
    d_queries, d_resp_kv, part_k = pl.pallas_call(
        functools.partial(query_key_kernel, owners),
        out_shape=(
            jax.ShapeDtypeStruct((RESP_DEV * RLEN, HEADS * HD), bf16),
            jax.ShapeDtypeStruct((RESP_DEV * RLEN, 2 * HD), bf16),
            part_shape,
        ),
        in_specs=[vmem(), vmem(), vmem(), hbm(), vmem()],
        out_specs=[vmem()] * 3,
        scratch_shapes=[
            pltpu.VMEM((RESP_DEV, keys, ROWS), bf16),
            pltpu.SemaphoreType.DMA((RESP_DEV,)),
        ],
        compiler_params=params(),
        name="query_key",
    )(queries[0], resp_kv[0], fetched, in_hbm(score_grad), down_v)

    rows, prompt_rows = RESP_DEV * RLEN, slot_rows * PB
    width = resp_inputs.shape[2]
    half = width // 2
    resp_in = resp_inputs[0]
    prompt_in = prompt_inputs[0].reshape(prompt_rows, width)

    d_value, sent = pl.pallas_call(
        functools.partial(combine_kernel, owners),
        out_shape=(
            jax.ShapeDtypeStruct((prompt_rows, HD), bf16),
            jax.ShapeDtypeStruct((half, HD), bf16),
        ),
        in_specs=[smem()] * 3 + [vmem()] * 4,
        out_specs=[vmem()] * 2,
        scratch_shapes=[
            pltpu.SMEM((blocks.shape[0],), jnp.int32),
            pltpu.VMEM((slot_rows, PB, HD), f32),
        ],
        compiler_params=params(),
        name="combine",
    )(pos, blocks, order, returned_v, resp_in, down_v, prompt_in)
    swap = [(i, i ^ 1) for i in range(owners)]
    from_twin = lax.ppermute(sent, "seq", swap)
    kept = pl.pallas_call(
        weight_kernel,
        out_shape=jax.ShapeDtypeStruct((half, HD), bf16),
        in_specs=[smem()] + [vmem()] * 4,
        out_specs=vmem(),
        compiler_params=params(),
        name="weights",
    )(pos, resp_in, down_v, prompt_in, d_value)

    both = (kept.astype(f32) + from_twin.astype(f32)).astype(bf16)
    twins = [list(range(c, owners, 2)) for c in range(2)]
    chips = owners // 2
    shares = lax.all_to_all(both, "seq", 0, 0, tiled=True, axis_index_groups=twins)
    share = jnp.sum(shares.reshape(chips, half // chips, HD).astype(f32), axis=0)
    share, part_k = lax.optimization_barrier((share, part_k))
    returned_k = to_owners(part_k)
    key_total = grp_count * owners * (rows + prompt_rows)
    share = (grp_sum(share, grp_count) * key_total ** (-0.5)).astype(bf16)
    share, returned_k = lax.optimization_barrier((share, returned_k))
    copies = jnp.broadcast_to(share[None], (chips,) + share.shape).reshape(half, HD)
    mine = lax.all_to_all(copies, "seq", 0, 0, tiled=True, axis_index_groups=twins)
    theirs = lax.ppermute(mine, "seq", swap)
    d_value_weight = pl.pallas_call(
        finish_kernel,
        out_shape=pltpu.HBM((width, HD), bf16),
        in_specs=[smem(), vmem(), vmem()],
        out_specs=hbm(),
        scratch_shapes=[pltpu.SemaphoreType.DMA((2,))],
        compiler_params=params(),
        name="finish",
    )(pos, mine, theirs)
    d_prompt = pl.pallas_call(
        functools.partial(join_kernel, owners),
        out_shape=jax.ShapeDtypeStruct((prompt_rows, 2 * HD), bf16),
        in_specs=[smem()] * 3 + [vmem()] * 2,
        out_specs=vmem(),
        scratch_shapes=[
            pltpu.SMEM(blocks.shape, jnp.int32),
            pltpu.VMEM((slot_rows, PB, HD), f32),
        ],
        compiler_params=params(),
        name="join",
    )(pos, blocks, order, returned_k, d_value)
    d_prompt = d_prompt.reshape(slot_rows, PB, 2 * HD)
    return (d_queries[None], d_resp_kv[None], d_prompt[None], d_value_weight)


def solution(mesh):
    in_specs = (
        P("grp", "seq", None),
        P("grp", "seq", None),
        P("grp", "seq", None),
        P("grp", None, "seq", None),
        P("grp", "seq", None),
        P("grp", None, "seq", None),
        P("grp", None),
        P("grp", None),
        P("grp", "seq"),
    )
    out_specs = (P("grp", "seq", None), P("grp", "seq", None), P("grp", None, "seq", None), P())
    return jax.shard_map(local, mesh=mesh, in_specs=in_specs, out_specs=out_specs, check_vma=False)
```

```python
import functools

import jax
import jax.numpy as jnp
from jax import lax
from jax.experimental import pallas as pl
from jax.experimental.pallas import tpu as pltpu
from jax.sharding import PartitionSpec as P

HD = 128
HEADS = 5
RLEN = 64
RESP_DEV = 2
RPP = 8
PB = 64
ROWS = HEADS * RLEN
SCALING = HD ** (-0.5)
LOG2E = 1.4426950408889634
OWN_BLOCKS = 4
CHUNK = 640
NT = (((1,), (1,)), ((), ()))
TN = (((0,), (0,)), ((), ()))


def first_block(blocks_ref, prompt):
    total = jnp.int32(0)
    for i in range(blocks_ref.shape[0]):
        total = total + jnp.where(i < prompt, blocks_ref[i], 0)
    return total


def fill_starts(blocks_ref, starts_ref):
    total = jnp.int32(0)
    for i in range(blocks_ref.shape[0]):
        starts_ref[i] = total
        total = total + blocks_ref[i]


def place_of(response, owner, order_ref, starts_ref, owners, slot_rows):
    begin = starts_ref[order_ref[response] >> 3]
    offset = (owner - begin) & (owners - 1)
    return jnp.minimum((begin + offset) >> (owners.bit_length() - 1), slot_rows - 1)


def pack_kernel(
    owners,
    pos_ref,
    blocks_hbm,
    order_hbm,
    kv_hbm,
    out_ref,
    blocks_ref,
    order_ref,
    starts_ref,
    kv_ref,
    sems,
):
    copies = [
        pltpu.make_async_copy(blocks_hbm.at[0], blocks_ref, sems.at[0]),
        pltpu.make_async_copy(order_hbm.at[0], order_ref, sems.at[1]),
        pltpu.make_async_copy(kv_hbm.at[0], kv_ref, sems.at[2]),
    ]
    for copy in copies:
        copy.start()
    for copy in copies:
        copy.wait()
    fill_starts(blocks_ref, starts_ref)
    owner = pos_ref[0]

    def body(response, carry):
        place = place_of(response, owner, order_ref, starts_ref, owners, kv_ref.shape[0])
        out_ref[response] = kv_ref[place]
        return carry

    lax.fori_loop(0, out_ref.shape[0], body, 0, unroll=8)


def attention_kernel(
    owners,
    pos_ref,
    blocks_ref,
    order_ref,
    len_ref,
    query_ref,
    own_ref,
    grad_ref,
    got_ref,
    dq_ref,
    down_ref,
    down_v_ref,
    back_k_hbm,
    back_v_ref,
    score_ref,
    pgrad_ref,
    back_k_ref,
    sems,
):
    f32, bf16 = jnp.float32, jnp.bfloat16
    chunk = OWN_BLOCKS * PB
    chunks = owners // OWN_BLOCKS
    factor = SCALING * LOG2E
    copies = []
    for member in range(RESP_DEV):
        prompt = order_ref[pos_ref[0] * RESP_DEV + member] >> 3
        begin = first_block(blocks_ref, prompt)
        count = blocks_ref[prompt]
        rows = slice(member * RLEN, (member + 1) * RLEN)
        q = jnp.concatenate(
            [query_ref[rows, h * HD : (h + 1) * HD] for h in range(HEADS)], axis=0
        )
        g = jnp.concatenate([grad_ref[rows, h * HD : (h + 1) * HD] for h in range(HEADS)], axis=0)
        row_ids = lax.broadcasted_iota(jnp.int32, (ROWS, HD), 0) & (RLEN - 1)
        g = jnp.where(row_ids < len_ref[member], g, jnp.zeros_like(g))

        def keys_of(i):
            if i < chunks:
                part = got_ref[i * OWN_BLOCKS : (i + 1) * OWN_BLOCKS, member]
                return part.reshape(chunk, 2 * HD)
            return own_ref[rows, :]

        def rows_of(i):
            return slice(i * chunk, i * chunk + (chunk if i < chunks else RLEN))

        top = jnp.full((8, ROWS), -1e30, f32)
        for i in range(chunks + 1):
            kv = keys_of(i)
            s = lax.dot_general(kv[:, :HD], q, NT, preferred_element_type=f32)
            if i < chunks:
                seen = []
                for j in range(OWN_BLOCKS):
                    offset = (i * OWN_BLOCKS + j - begin) & (owners - 1)
                    hidden = jnp.where(offset < count, 0.0, -1e30)
                    seen.append(s[j * PB : (j + 1) * PB] + hidden)
                s = jnp.concatenate(seen, axis=0)
            else:
                key_ids = lax.broadcasted_iota(jnp.int32, s.shape, 0)
                query_ids = lax.broadcasted_iota(jnp.int32, s.shape, 1) & (RLEN - 1)
                s = jnp.where(key_ids <= query_ids, s, -1e30)
            score_ref[rows_of(i), :] = s
            top = jnp.maximum(top, jnp.max(s.reshape(-1, 8, ROWS), axis=0))
        top = jnp.max(top, axis=0, keepdims=True)
        total = jnp.zeros((8, ROWS), f32)
        mixed = jnp.zeros((8, ROWS), f32)
        for i in range(chunks + 1):
            kv = keys_of(i)
            pg = lax.dot_general(kv[:, HD:], g, NT, preferred_element_type=f32)
            e = jnp.exp2((score_ref[rows_of(i), :] - top) * factor)
            score_ref[rows_of(i), :] = e
            pgrad_ref[rows_of(i), :] = pg
            total = total + jnp.sum(e.reshape(-1, 8, ROWS), axis=0)
            mixed = mixed + jnp.sum((e * pg).reshape(-1, 8, ROWS), axis=0)
        inverse = 1.0 / jnp.sum(total, axis=0, keepdims=True)
        row_total = jnp.sum(mixed, axis=0, keepdims=True) * inverse
        dqt = jnp.zeros((HD, ROWS), f32)
        for i in range(chunks + 1):
            kv = keys_of(i)
            p = score_ref[rows_of(i), :] * inverse
            ds = (p * (pgrad_ref[rows_of(i), :] - row_total)).astype(bf16)
            dk = lax.dot_general(ds, q, (((1,), (0,)), ((), ())), preferred_element_type=f32)
            dv = lax.dot_general(
                p.astype(bf16), g, (((1,), (0,)), ((), ())), preferred_element_type=f32
            )
            dk, dv = (dk * SCALING).astype(bf16), dv.astype(bf16)
            if i < chunks:
                part = slice(i * OWN_BLOCKS, (i + 1) * OWN_BLOCKS)
                back_k_ref[member, part] = dk.reshape(OWN_BLOCKS, PB, HD)
                back_v_ref[part, member] = dv.reshape(OWN_BLOCKS, PB, HD)
            else:
                down_ref[rows, :HD] = dk
                down_ref[rows, HD:] = dv
                down_v_ref[rows, :] = dv
            dqt = dqt + lax.dot_general(kv[:, :HD], ds, TN, preferred_element_type=f32)
        copies.append(
            pltpu.make_async_copy(back_k_ref.at[member], back_k_hbm.at[:, member], sems.at[member])
        )
        copies[-1].start()
        dq = (dqt * SCALING).T.astype(bf16)
        for h in range(HEADS):
            dq_ref[rows, h * HD : (h + 1) * HD] = dq[h * RLEN : (h + 1) * RLEN]
    for copy in copies:
        copy.wait()


def some_weights(start, resp_in_ref, resp_grad, prompt_in_ref, prompt_grad, weight_ref):
    for i in range(weight_ref.shape[0] // CHUNK):
        place = pl.ds(pl.multiple_of(start + i * CHUNK, HD), CHUNK)
        term = lax.dot_general(
            resp_in_ref[:, place], resp_grad, TN, preferred_element_type=jnp.float32
        )
        more = lax.dot_general(
            prompt_in_ref[:, place], prompt_grad, TN, preferred_element_type=jnp.float32
        )
        weight_ref[i * CHUNK : (i + 1) * CHUNK, :] = (term + more).astype(jnp.bfloat16)


def sum_blocks(owners, pos_ref, blocks_ref, order_ref, got_ref, starts_ref, acc_ref):
    fill_starts(blocks_ref, starts_ref)
    owner = pos_ref[0]
    acc_ref[...] = jnp.zeros_like(acc_ref)

    def body(response, carry):
        place = place_of(response, owner, order_ref, starts_ref, owners, acc_ref.shape[0])
        acc_ref[place] += got_ref[response].astype(jnp.float32)
        return carry

    lax.fori_loop(0, got_ref.shape[0], body, 0, unroll=8)


def combine_kernel(
    owners,
    pos_ref,
    blocks_ref,
    order_ref,
    got_ref,
    resp_in_ref,
    resp_grad_ref,
    prompt_in_ref,
    out_ref,
    weight_ref,
    starts_ref,
    acc_ref,
):
    sum_blocks(owners, pos_ref, blocks_ref, order_ref, got_ref, starts_ref, acc_ref)
    prompt_grad = acc_ref[...].reshape(out_ref.shape).astype(jnp.bfloat16)
    out_ref[...] = prompt_grad
    other = 1 - (pos_ref[0] & 1)
    start = other * (resp_in_ref.shape[1] // 2)
    some_weights(start, resp_in_ref, resp_grad_ref[...], prompt_in_ref, prompt_grad, weight_ref)


def join_kernel(
    owners, pos_ref, blocks_ref, order_ref, got_ref, value_ref, out_ref, starts_ref, acc_ref
):
    sum_blocks(owners, pos_ref, blocks_ref, order_ref, got_ref, starts_ref, acc_ref)
    out_ref[:, :HD] = acc_ref[...].reshape(value_ref.shape).astype(jnp.bfloat16)
    out_ref[:, HD:] = value_ref[...]


def weight_kernel(
    flip, offset, pos_ref, resp_in_ref, resp_grad_ref, prompt_in_ref, prompt_grad_ref, weight_ref
):
    some_weights(
        ((pos_ref[0] & 1) ^ flip) * (resp_in_ref.shape[1] // 2) + offset,
        resp_in_ref,
        resp_grad_ref[...],
        prompt_in_ref,
        prompt_grad_ref[...],
        weight_ref,
    )


def finish_kernel(pos_ref, mine_ref, theirs_ref, out_hbm, sems):
    half = mine_ref.shape[0]
    core = pos_ref[0] & 1
    copies = [
        pltpu.make_async_copy(
            source, out_hbm.at[pl.ds(pl.multiple_of(place * half, half), half)], sems.at[i]
        )
        for i, (source, place) in enumerate(((mine_ref, core), (theirs_ref, 1 - core)))
    ]
    for copy in copies:
        copy.start()
    for copy in copies:
        copy.wait()


def smem():
    return pl.BlockSpec(memory_space=pltpu.SMEM)


def vmem():
    return pl.BlockSpec(memory_space=pltpu.VMEM)


def hbm():
    return pl.BlockSpec(memory_space=pltpu.HBM)


def in_hbm(x):
    return pltpu.with_memory_space_constraint(x, pltpu.HBM)


def params():
    return pltpu.CompilerParams(vmem_limit_bytes=20 * 1024 * 1024)


def grp_sum(part, grp_count):
    total, step = part, 1
    while step < grp_count:
        width = min(4, grp_count // step)
        own = total.astype(jnp.bfloat16)
        terms = [own.astype(jnp.float32)]
        for k in range(1, width):
            pairs = [(i, i ^ (k * step)) for i in range(grp_count)]
            terms.append(lax.ppermute(own, "grp", pairs).astype(jnp.float32))
        while len(terms) > 1:
            terms = [terms[i] + terms[i + 1] for i in range(0, len(terms), 2)]
        total, step = terms[0], step * width
    return total


def local(
    queries,
    resp_kv,
    grad_out,
    prompt_kv,
    resp_inputs,
    prompt_inputs,
    prompt_blocks,
    response_order,
    response_len,
):
    bf16, f32 = jnp.bfloat16, jnp.float32
    owners = lax.axis_size("seq")
    grp_count = lax.axis_size("grp")
    slot_rows = prompt_kv.shape[1]
    responses = owners * RESP_DEV
    pos = lax.axis_index("seq").astype(jnp.int32).reshape(1)
    blocks, order, lengths = prompt_blocks[0], response_order[0], response_len[0]

    packed = pl.pallas_call(
        functools.partial(pack_kernel, owners),
        out_shape=jax.ShapeDtypeStruct((responses, PB, 2 * HD), bf16),
        in_specs=[smem()] + [pl.BlockSpec(memory_space=pltpu.HBM)] * 3,
        out_specs=vmem(),
        scratch_shapes=[
            pltpu.SMEM(blocks.shape, jnp.int32),
            pltpu.SMEM(order.shape, jnp.int32),
            pltpu.SMEM(blocks.shape, jnp.int32),
            pltpu.VMEM(prompt_kv.shape[1:2] + (PB, 2 * HD), bf16),
            pltpu.SemaphoreType.DMA((3,)),
        ],
        compiler_params=params(),
        name="pack",
    )(pos, in_hbm(prompt_blocks), in_hbm(response_order), in_hbm(prompt_kv))
    fetched = lax.all_to_all(
        packed.reshape(responses * PB, 2 * HD), "seq", 0, 0, tiled=True
    ).reshape(owners, RESP_DEV, PB, 2 * HD)

    keys = owners * PB + RLEN
    part_shape = jax.ShapeDtypeStruct((owners, RESP_DEV, PB, HD), bf16)
    d_queries, d_resp_kv, d_value_own, part_k, part_v = pl.pallas_call(
        functools.partial(attention_kernel, owners),
        out_shape=(
            jax.ShapeDtypeStruct((RESP_DEV * RLEN, HEADS * HD), bf16),
            jax.ShapeDtypeStruct((RESP_DEV * RLEN, 2 * HD), bf16),
            jax.ShapeDtypeStruct((RESP_DEV * RLEN, HD), bf16),
            pltpu.HBM(part_shape.shape, bf16),
            part_shape,
        ),
        in_specs=[smem()] * 4 + [vmem()] * 4,
        out_specs=[vmem(), vmem(), vmem(), hbm(), vmem()],
        scratch_shapes=[
            pltpu.VMEM((keys, ROWS), f32),
            pltpu.VMEM((keys, ROWS), f32),
            pltpu.VMEM((RESP_DEV, owners, PB, HD), bf16),
            pltpu.SemaphoreType.DMA((RESP_DEV,)),
        ],
        compiler_params=params(),
        name="attention",
    )(pos, blocks, order, lengths, queries[0], resp_kv[0], grad_out[0], fetched)
    def to_owners(part):
        got = lax.all_to_all(part.reshape(responses * PB, HD), "seq", 0, 0, tiled=True)
        return got.reshape(responses, PB, HD)

    returned_v = to_owners(part_v)

    rows, prompt_rows = RESP_DEV * RLEN, slot_rows * PB
    width = resp_inputs.shape[2]
    half = width // 2
    resp_in = resp_inputs[0]
    prompt_in = prompt_inputs[0].reshape(prompt_rows, width)

    d_value, sent = pl.pallas_call(
        functools.partial(combine_kernel, owners),
        out_shape=(
            jax.ShapeDtypeStruct((prompt_rows, HD), bf16),
            jax.ShapeDtypeStruct((half // 2, HD), bf16),
        ),
        in_specs=[smem()] * 3 + [vmem()] * 4,
        out_specs=[vmem()] * 2,
        scratch_shapes=[
            pltpu.SMEM((blocks.shape[0],), jnp.int32),
            pltpu.VMEM((slot_rows, PB, HD), f32),
        ],
        compiler_params=params(),
        name="combine",
    )(pos, blocks, order, returned_v, resp_in, d_value_own, prompt_in)
    swap = [(i, i ^ 1) for i in range(owners)]

    def weights(flip, offset, count):
        return pl.pallas_call(
            functools.partial(weight_kernel, flip, offset),
            out_shape=jax.ShapeDtypeStruct((count, HD), bf16),
            in_specs=[smem()] + [vmem()] * 4,
            out_specs=vmem(),
            compiler_params=params(),
            name="weights",
        )(pos, resp_in, d_value_own, prompt_in, d_value)

    more = weights(1, half // 2, half // 2)
    swap = [(i, i ^ 1) for i in range(owners)]
    from_twin = [lax.ppermute(x, "seq", swap) for x in (sent, more)]
    kept = weights(0, 0, half)
    both = (kept.astype(f32) + jnp.concatenate(from_twin, axis=0).astype(f32)).astype(bf16)
    twins = [list(range(c, owners, 2)) for c in range(2)]
    chips = owners // 2
    shares = lax.all_to_all(both, "seq", 0, 0, tiled=True, axis_index_groups=twins)
    share = jnp.sum(shares.reshape(chips, half // chips, HD).astype(f32), axis=0)
    share, part_k = lax.optimization_barrier((share, part_k))
    returned_k = to_owners(part_k)
    key_total = grp_count * owners * (rows + prompt_rows)
    share = (grp_sum(share, grp_count) * key_total ** (-0.5)).astype(bf16)
    share, returned_k = lax.optimization_barrier((share, returned_k))
    copies = jnp.broadcast_to(share[None], (chips,) + share.shape).reshape(half, HD)
    mine = lax.all_to_all(copies, "seq", 0, 0, tiled=True, axis_index_groups=twins)
    theirs = lax.ppermute(mine, "seq", swap)
    d_value_weight = pl.pallas_call(
        finish_kernel,
        out_shape=pltpu.HBM((width, HD), bf16),
        in_specs=[smem(), vmem(), vmem()],
        out_specs=hbm(),
        scratch_shapes=[pltpu.SemaphoreType.DMA((2,))],
        compiler_params=params(),
        name="finish",
    )(pos, mine, theirs)
    d_prompt = pl.pallas_call(
        functools.partial(join_kernel, owners),
        out_shape=jax.ShapeDtypeStruct((prompt_rows, 2 * HD), bf16),
        in_specs=[smem()] * 3 + [vmem()] * 2,
        out_specs=vmem(),
        scratch_shapes=[
            pltpu.SMEM(blocks.shape, jnp.int32),
            pltpu.VMEM((slot_rows, PB, HD), f32),
        ],
        compiler_params=params(),
        name="join",
    )(pos, blocks, order, returned_k, d_value)
    d_prompt = d_prompt.reshape(slot_rows, PB, 2 * HD)
    return (d_queries[None], d_resp_kv[None], d_prompt[None], d_value_weight)


def solution(mesh):
    in_specs = (
        P("grp", "seq", None),
        P("grp", "seq", None),
        P("grp", "seq", None),
        P("grp", None, "seq", None),
        P("grp", "seq", None),
        P("grp", None, "seq", None),
        P("grp", None),
        P("grp", None),
        P("grp", "seq"),
    )
    out_specs = (P("grp", "seq", None), P("grp", "seq", None), P("grp", None, "seq", None), P())
    return jax.shard_map(local, mesh=mesh, in_specs=in_specs, out_specs=out_specs, check_vma=False)
```
